32 devices in a mesh: rep: 2 (over y), seq: 4 (over z), tp: 4 (over x, core).
Axes of the slice: x: 2, y: 2, z: 4, core: 2. Of those that a mesh axis runs over, the one named last changes fastest.
Arguments:
- queries: bfloat16 [2048, 8192], P(('rep', 'seq'), 'tp'), parts along dimension 0, may hold values from -9 to 9
- keys: bfloat16 [2048, 1024], P(('rep', 'seq'), 'tp'), parts along dimension 0, may hold values from -9 to 9
- values: bfloat16 [2048, 1024], P(('rep', 'seq'), 'tp'), parts along dimension 0, may hold values from -6 to 6
- segments: int32 [2048], P(('rep', 'seq')), parts along dimension 0, may hold values from 0 to 15, as said below
Outputs:
- attended: bfloat16 [2048, 8192], P(('rep', 'seq'), 'tp'), parts along dimension 0
The draws below stay inside these ranges and needn't reach their ends.
There are 2 independent parts, one for each index of `rep`. The reference program is written for one: setup_inputs(seed, part) draws one part's arguments, and reference() takes and returns one part's arrays. A program takes and returns all parts, laid end to end along the dimension named above; each array names one. Nothing has to cross between parts.
Inputs may be any that keep to these rules, and one draw needn't show every extreme that they name: `segments`: segment numbers never fall and each of the 16 documents has at least one token; document 0 is the longest, its 640 tokens are the first ones of the sequence; document 1 follows with exactly 192 tokens; the others have at most 1024 - 640 tokens each.
All inputs are finite; a program needn't handle non-finite values.
Results may differ from the reference program's by a relative error of at most 0.0075.
Values may be sent and summed in bfloat16 or wider, within the bound.
A program may use at most 64 MiB of HBM per device.

```python
import math
import jax
import jax.numpy as jnp
from jax import lax

HEADS = 64
KV_HEADS = 8
HEAD_DIM = 128
TOK_DEV = 256
DOCS = 16
TOKENS = 1024
DOC_MAX = 640


def draw_queries(key, part):
    own_key = jax.random.fold_in(key, 11)
    normal_part = jax.random.truncated_normal(own_key, -3.6, 3.6, (TOKENS, HEADS * HEAD_DIM), jnp.float32)
    return (2.5 * normal_part).astype(jnp.bfloat16)


def draw_keys(key, part):
    own_key = jax.random.fold_in(key, 23)
    return jax.random.truncated_normal(own_key, -6.0, 6.0, (TOKENS, KV_HEADS * HEAD_DIM), jnp.float32).astype(jnp.bfloat16)


def draw_segments(key, part):
    own_key = jax.random.fold_in(key, 37)
    remain = TOKENS - DOC_MAX
    first_length = 3 * TOK_DEV // 4
    shuffled = jax.random.permutation(own_key, remain - first_length - 1) + first_length + 1
    cuts = jnp.concatenate([jnp.full((1,), first_length, jnp.int32), shuffled[:DOCS - 3].astype(jnp.int32)])
    position = jnp.arange(TOKENS, dtype=jnp.int32)
    offset = position - DOC_MAX
    later = 1 + jnp.sum((cuts[None, :] <= offset[:, None]).astype(jnp.int32), axis=1)
    return jnp.where(position < DOC_MAX, 0, later).astype(jnp.int32)


def block_scale(rng, extent, shards, least, largest):
    def one(dim, shards_of):
        heights = jax.random.uniform(jax.random.fold_in(jax.random.fold_in(rng, 6), dim), (shards_of,), jnp.float32, least / len(shards), largest / len(shards))
        return jnp.repeat(jnp.exp(heights), extent[dim] // shards_of).reshape((-1,) + (1,) * (len(extent) - dim - 1))

    loudness = one(*shards[0])
    for cut in shards[1:]:
        loudness = loudness * one(*cut)
    return loudness


def normal_values(key, extent, deviation, reach, cuts=(), kind=jnp.bfloat16):
    result = deviation * jax.random.normal(key, extent, jnp.float32)
    if cuts:
        result = result * block_scale(key, extent, cuts, -0.22, 0.18)
    return jnp.clip(result, -reach, reach).astype(kind)


def setup_inputs(seed: int = 0, part: int = 0) -> dict:
    splits = jax.random.split(jax.random.key(seed), 5)
    part_keys = jax.random.split(jax.random.fold_in(splits[4], part), 5)
    queries = draw_queries(jax.random.fold_in(jax.random.fold_in(splits[4], part), 71), part)
    keys = draw_keys(jax.random.fold_in(jax.random.fold_in(splits[4], part), 71), part)
    values = normal_values(part_keys[2], (TOKENS, KV_HEADS * HEAD_DIM), 1.0, 6.0, ((0, 4), (1, 4)))
    segments = draw_segments(jax.random.fold_in(jax.random.fold_in(splits[4], part), 71), part)
    return {"queries": queries, "keys": keys, "values": values, "segments": segments}


def rotate(rows_in, places, width):
    row_count = rows_in.shape[0]
    head_count = rows_in.shape[1] // width
    half_width = width // 2
    vectors = rows_in.astype(jnp.float32).reshape(row_count, head_count, width)
    frequency = 1000000.0 ** (-jnp.arange(half_width, dtype=jnp.float32) / half_width)
    angles = places.astype(jnp.float32)[:, None] * frequency[None, :]
    cos_part = jnp.cos(angles)[:, None, :]
    sin_part = jnp.sin(angles)[:, None, :]
    lower_half = vectors[..., :half_width]
    upper_half = vectors[..., half_width:]
    turned = jnp.concatenate([lower_half * cos_part - upper_half * sin_part, upper_half * cos_part + lower_half * sin_part], axis=-1)
    return turned.astype(jnp.bfloat16)

def doc_places(segments):
    member = (segments[:, None] == jnp.arange(DOCS, dtype=jnp.int32)[None, :]).astype(jnp.int32)
    totals = lax.optimization_barrier(jnp.sum(member, axis=0))
    starts = jnp.cumsum(totals) - totals
    return jnp.arange(TOKENS, dtype=jnp.int32) - lax.optimization_barrier(jnp.sum(member * starts[None, :], axis=1))

def reference(queries, keys, values, segments):
    places = doc_places(segments)
    group_size = HEADS // KV_HEADS
    scale_factor = 1.0 / math.sqrt(HEAD_DIM)
    block = math.gcd(TOKENS, 512)
    block_count = TOKENS // block
    query_rot = rotate(queries, places, HEAD_DIM).reshape(block_count, block, KV_HEADS, group_size, HEAD_DIM)
    query_split = jnp.transpose(query_rot, (2, 0, 3, 1, 4))
    key_split = jnp.transpose(rotate(keys, places, HEAD_DIM), (1, 0, 2))
    value_split = jnp.transpose(values.reshape(TOKENS, KV_HEADS, HEAD_DIM), (1, 0, 2))
    key_index = jnp.arange(TOKENS, dtype=jnp.int32)

    def per_head(operands):
        query_head, key_head, value_head = operands
        key_wide = key_head.astype(jnp.float32)
        value_wide = value_head.astype(jnp.float32)

        def per_block(inputs):
            query_block, block_id = inputs
            query_index = block_id * block + jnp.arange(block, dtype=jnp.int32)
            query_seg = lax.dynamic_slice_in_dim(segments, (block_id * block).astype(jnp.int32), block)
            allowed = (key_index[None, :] <= query_index[:, None]) & (segments[None, :] == query_seg[:, None])
            scores = jnp.einsum('gqd,td->gqt', query_block.astype(jnp.float32), key_wide) * scale_factor
            scores = jnp.where(allowed[None], scores, -1e+30)
            row_max = lax.optimization_barrier(jnp.max(scores, axis=-1, keepdims=True))
            weights = jnp.where(allowed[None], jnp.exp(scores - row_max), 0.0)
            total = lax.optimization_barrier(jnp.sum(weights, axis=-1, keepdims=True))
            rounded = lax.optimization_barrier(weights.astype(jnp.bfloat16)).astype(jnp.float32)
            mixed = jnp.einsum('gqt,td->gqd', rounded, value_wide)
            return (mixed / total).astype(jnp.bfloat16)
        return lax.map(per_block, (query_head, jnp.arange(block_count, dtype=jnp.int32)))
    outcome = lax.map(per_head, (query_split, key_split, value_split))
    outcome = jnp.transpose(outcome, (1, 3, 0, 2, 4))
    return outcome.reshape(TOKENS, HEADS * HEAD_DIM)
```

```python
import functools
import math

import jax
import jax.numpy as jnp
from jax import lax
from jax.experimental import pallas as pl
from jax.experimental.pallas import tpu as pltpu
from jax.sharding import PartitionSpec as P

HEAD_DIM = 128
HALF = 128
SECOND_DOC = 192
MASKED = -1e30
EXPONENT = math.log2(math.e) / math.sqrt(HEAD_DIM)
MESH = pl.DeviceIdType.MESH


def first_key_block(tile, doc0):
    later = jnp.where(tile < (doc0 + SECOND_DOC) // HALF + 1, doc0 // HALF, (doc0 + SECOND_DOC) // HALF)
    return jnp.where(tile < doc0 // HALF, 0, later)


def kernel(
    n, doc0, has_before, q_ref, k_ref, v_ref, seg_ref, *refs
):
    before_ref = refs[0] if has_before else None
    (
    out_ref, k_all, v_all, q_rot, acc, top, total, cos_ref, sin_ref, start_ref,
    send_sem, recv_sem, own_sem,
    ) = refs[has_before:]
    me = lax.axis_index("seq")
    rows = k_ref.shape[0]
    halves = rows // HALF
    kv_heads = k_ref.shape[1] // HEAD_DIM
    group = q_ref.shape[1] // k_ref.shape[1]
    first_row = me * rows

    barrier = pltpu.get_barrier_semaphore()
    for step in range(1, n):
        pl.semaphore_signal(
            barrier, inc=1, device_id={"seq": lax.rem(me + step, n)}, device_id_type=MESH
        )

    def first_source(device):
        low = first_key_block(device * halves, doc0)
        for half in range(1, halves):
            low = jnp.minimum(low, first_key_block(device * halves + half, doc0))
        return low // halves

    def wanted(step):
        other = me + step
        return (other < n) & (me >= first_source(other))

    def send(step, kind):
        source = v_ref if kind else k_all.at[me]
        target = v_all.at[me] if kind else k_all.at[me]
        return pltpu.make_async_remote_copy(
            src_ref=source,
            dst_ref=target,
            send_sem=send_sem.at[step, kind],
            recv_sem=recv_sem.at[step, kind],
            device_id={"seq": lax.rem(me + step, n)},
            device_id_type=MESH,
        )

    own_v = pltpu.make_async_copy(v_ref, v_all.at[me], own_sem)
    own_v.start()
    pl.semaphore_wait(barrier, n - 1)

    for step in range(1, n):
        @pl.when(wanted(step))
        def _():
            send(step, 1).start()

    seg_row = jnp.broadcast_to(seg_ref[...], (rows, rows))
    earlier = (seg_row < seg_row.T).astype(jnp.float32)
    local_before = jnp.sum(earlier, axis=1, keepdims=True).astype(jnp.int32)
    token = first_row + lax.broadcasted_iota(jnp.int32, (rows, 1), 0)
    start = first_row + local_before
    if has_before:
        start = jnp.where(local_before == 0, before_ref[0, 0], start)
    start = jnp.where(token < doc0, 0, jnp.where(token < doc0 + SECOND_DOC, doc0, start))
    start_ref[...] = start
    lane = lax.broadcasted_iota(jnp.int32, (1, HEAD_DIM), 1)
    index = (lane % (HEAD_DIM // 2)).astype(jnp.float32)
    frequency = jnp.exp(index * (-math.log(1000000.0) / (HEAD_DIM // 2)))
    angles = (token - start).astype(jnp.float32) * frequency
    cos_ref[...] = jnp.cos(angles)
    sin_ref[...] = jnp.where(lane < HEAD_DIM // 2, -1.0, 1.0) * jnp.sin(angles)

    def turn(x, cos_part, sin_part):
        wide = x.astype(jnp.float32)
        swapped = pltpu.roll(wide, HEAD_DIM // 2, 1)
        return (wide * cos_part + swapped * sin_part).astype(jnp.bfloat16)

    for head in range(kv_heads):
        columns = slice(head * HEAD_DIM, (head + 1) * HEAD_DIM)
        k_all[me, :, columns] = turn(k_ref[:, columns], cos_ref[...], sin_ref[...])
    for step in range(1, n):
        @pl.when(wanted(step))
        def _():
            send(step, 0).start()

    for half in range(halves):
        part = slice(half * HALF, (half + 1) * HALF)
        for head in range(kv_heads * group):
            columns = slice(head * HEAD_DIM, (head + 1) * HEAD_DIM)
            q_rot[half, head] = turn(q_ref[part, columns], cos_ref[part], sin_ref[part])

    def scores(half, kv, head, source, upto, allowed):
        columns = slice(kv * HEAD_DIM, (kv + 1) * HEAD_DIM)
        found = lax.dot_general(
            q_rot[half, head],
            k_all[source, :upto, columns],
            (((1,), (1,)), ((), ())),
            preferred_element_type=jnp.float32,
        )
        return jnp.where(allowed, found, MASKED)

    def mask(half, source, upto):
        part = slice(half * HALF, (half + 1) * HALF)
        key = source * rows + lax.broadcasted_iota(jnp.int32, (1, upto), 1)
        query = first_row + half * HALF + lax.broadcasted_iota(jnp.int32, (HALF, 1), 0)
        return (key >= start_ref[part]) & (key <= query)

    own_v.wait()
    for half in range(halves):
        upto = (half + 1) * HALF
        allowed = mask(half, me, upto)
        for head in range(kv_heads * group):
            kv = head // group
            columns = slice(kv * HEAD_DIM, (kv + 1) * HEAD_DIM)
            found = scores(half, kv, head, me, upto, allowed)
            peak = jnp.max(found, axis=1, keepdims=True)
            weight = jnp.exp2((found - peak) * EXPONENT)
            top[half, head] = peak
            total[half, head] = jnp.sum(weight, axis=1, keepdims=True)
            acc[half, head] = jnp.dot(
                weight.astype(jnp.bfloat16),
                v_all[me, :upto, columns],
                preferred_element_type=jnp.float32,
            )

    def absorb(step, carry):
        source = me - step
        arrived = pltpu.make_async_remote_copy(
            src_ref=k_all.at[source], dst_ref=k_all.at[source],
            send_sem=send_sem.at[step, 0], recv_sem=recv_sem.at[step, 0],
            device_id={"seq": lax.rem(me + step, n)}, device_id_type=MESH,
        )
        arrived.wait_recv()
        arrived = pltpu.make_async_remote_copy(
            src_ref=v_all.at[source], dst_ref=v_all.at[source],
            send_sem=send_sem.at[step, 1], recv_sem=recv_sem.at[step, 1],
            device_id={"seq": lax.rem(me + step, n)}, device_id_type=MESH,
        )
        arrived.wait_recv()
        for half in range(halves):
            low = first_key_block(me * halves + half, doc0)

            @pl.when((source + 1) * halves > low)
            def _():
                allowed = mask(half, source, rows)
                for head in range(kv_heads * group):
                    kv = head // group
                    columns = slice(kv * HEAD_DIM, (kv + 1) * HEAD_DIM)
                    found = scores(half, kv, head, source, rows, allowed)
                    old = top[half, head]
                    peak = jnp.maximum(old, jnp.max(found, axis=1, keepdims=True))
                    weight = jnp.exp2((found - peak) * EXPONENT)
                    shrink = jnp.exp2((old - peak) * EXPONENT)
                    top[half, head] = peak
                    total[half, head] = total[half, head] * shrink + jnp.sum(
                        weight, axis=1, keepdims=True
                    )
                    acc[half, head] = acc[half, head] * shrink + jnp.dot(
                        weight.astype(jnp.bfloat16),
                        v_all[source, :, columns],
                        preferred_element_type=jnp.float32,
                    )
        return carry

    lax.fori_loop(1, me - first_source(me) + 1, absorb, 0)

    for half in range(halves):
        part = slice(half * HALF, (half + 1) * HALF)
        for head in range(kv_heads * group):
            columns = slice(head * HEAD_DIM, (head + 1) * HEAD_DIM)
            out_ref[part, columns] = (acc[half, head] / total[half, head]).astype(jnp.bfloat16)

    for step in range(1, n):
        @pl.when(wanted(step))
        def _():
            send(step, 1).wait_send()
            send(step, 0).wait_send()


def shards(n, queries, keys, values, segments):
    rows = queries.shape[0]
    tokens = n * rows
    doc0 = tokens // 2 + HALF
    kv_heads = keys.shape[1] // HEAD_DIM
    heads = queries.shape[1] // HEAD_DIM
    halves = rows // HALF
    operands = [queries, keys, values, segments.reshape(1, rows)]
    specs = [pl.BlockSpec(memory_space=pltpu.VMEM)] * 4
    has_before = (doc0 + SECOND_DOC) // rows < n - 1
    if has_before:
        every = lax.all_gather(segments, "seq", axis=0, tiled=True)
        before = jnp.sum((every < segments[0]).astype(jnp.int32))
        operands.append(before.reshape(1, 1))
        specs.append(pl.BlockSpec(memory_space=pltpu.SMEM))
    return pl.pallas_call(
        functools.partial(kernel, n, doc0, has_before),
        out_shape=jax.ShapeDtypeStruct(queries.shape, jnp.bfloat16),
        in_specs=specs,
        out_specs=pl.BlockSpec(memory_space=pltpu.VMEM),
        scratch_shapes=[
            pltpu.VMEM((n, rows, kv_heads * HEAD_DIM), jnp.bfloat16),
            pltpu.VMEM((n, rows, kv_heads * HEAD_DIM), jnp.bfloat16),
            pltpu.VMEM((halves, heads, HALF, HEAD_DIM), jnp.bfloat16),
            pltpu.VMEM((halves, heads, HALF, HEAD_DIM), jnp.float32),
            pltpu.VMEM((halves, heads, HALF, 1), jnp.float32),
            pltpu.VMEM((halves, heads, HALF, 1), jnp.float32),
            pltpu.VMEM((rows, HEAD_DIM), jnp.float32),
            pltpu.VMEM((rows, HEAD_DIM), jnp.float32),
            pltpu.VMEM((rows, 1), jnp.int32),
            pltpu.SemaphoreType.DMA((n, 2)),
            pltpu.SemaphoreType.DMA((n, 2)),
            pltpu.SemaphoreType.DMA,
        ],
        compiler_params=pltpu.CompilerParams(
            collective_id=0, has_side_effects=True, vmem_limit_bytes=48 * 1024 * 1024
        ),
    )(*operands)


def solution(mesh):
    placed = (
        P(("rep", "seq"), "tp"),
        P(("rep", "seq"), "tp"),
        P(("rep", "seq"), "tp"),
        P(("rep", "seq")),
    )
    return jax.shard_map(
        functools.partial(shards, mesh.shape["seq"]),
        mesh=mesh,
        in_specs=placed,
        out_specs=P(("rep", "seq"), "tp"),
        check_vma=False,
    )
```

```python
import functools
import math

import jax
import jax.numpy as jnp
from jax import lax
from jax.experimental import pallas as pl
from jax.experimental.pallas import tpu as pltpu
from jax.sharding import PartitionSpec as P

HEAD_DIM = 128
HALF = 128
SECOND_DOC = 192
MASKED = -1e30
EXPONENT = math.log2(math.e) / math.sqrt(HEAD_DIM)
MESH = pl.DeviceIdType.MESH


def first_key_block(tile, doc0):
    later = jnp.where(tile < (doc0 + SECOND_DOC) // HALF + 1, doc0 // HALF, (doc0 + SECOND_DOC) // HALF)
    return jnp.where(tile < doc0 // HALF, 0, later)


def kernel(
    n, doc0, has_before, q_hbm, k_hbm, v_hbm, seg_hbm, *refs
):
    before_ref = refs[0] if has_before else None
    (
        out_ref, q_ref, k_ref, seg_ref, k_all, v_all, q_rot, acc, top, total,
        cos_ref, sin_ref, start_ref, v_turned, weights, shrink, send_sem, recv_sem, own_sem,
    ) = refs[has_before:]
    me = lax.axis_index("seq")
    rows = k_hbm.shape[0]
    halves = rows // HALF
    kv_heads = k_hbm.shape[1] // HEAD_DIM
    group = q_hbm.shape[1] // k_hbm.shape[1]
    first_row = me * rows

    own = [
        pltpu.make_async_copy(source, target, own_sem.at[place])
        for place, (source, target) in enumerate(
            ((seg_hbm, seg_ref), (k_hbm, k_ref), (q_hbm, q_ref), (v_hbm, v_all.at[me]))
        )
    ]
    for copy in own:
        copy.start()

    barrier = pltpu.get_barrier_semaphore()

    def first_source(device):
        low = first_key_block(device * halves, doc0)
        for half in range(1, halves):
            low = jnp.minimum(low, first_key_block(device * halves + half, doc0))
        return low // halves

    def passed_on(source):
        return (me + 1 < n) & (source >= first_source(me + 1))

    def receives():
        return first_source(me) < me

    def send(step, kind):
        source = me - step
        held = (v_all if kind else k_all).at[source]
        return pltpu.make_async_remote_copy(
            src_ref=v_hbm if kind and isinstance(step, int) else held,
            dst_ref=held,
            send_sem=send_sem.at[step + 1, kind],
            recv_sem=recv_sem.at[step + 1, kind],
            device_id={"seq": lax.rem(me + 1, n)},
            device_id_type=MESH,
        )

    @pl.when(receives())
    def _():
        pl.semaphore_signal(
            barrier, inc=1, device_id={"seq": lax.rem(me - 1 + n, n)}, device_id_type=MESH
        )

    @pl.when(passed_on(me))
    def _():
        pl.semaphore_wait(barrier, 1)
        send(0, 1).start()

    own[0].wait()
    seg_row = jnp.broadcast_to(seg_ref[...], (rows, rows))
    seg_column = seg_row.T

    def document_start(token, earlier, axis):
        count = jnp.sum(earlier.astype(jnp.float32), axis=axis, keepdims=True).astype(jnp.int32)
        start = first_row + count
        if has_before:
            start = jnp.where(count == 0, before_ref[0, 0], start)
        return jnp.where(token < doc0, 0, jnp.where(token < doc0 + SECOND_DOC, doc0, start))

    token = first_row + lax.broadcasted_iota(jnp.int32, (1, rows), 1)
    start_ref[...] = document_start(token, seg_column < seg_row, 0)
    token = first_row + lax.broadcasted_iota(jnp.int32, (rows, 1), 0)
    start = document_start(token, seg_row < seg_column, 1)
    lane = lax.broadcasted_iota(jnp.int32, (1, HEAD_DIM), 1)
    index = (lane % (HEAD_DIM // 2)).astype(jnp.float32)
    frequency = jnp.exp(index * (-math.log(1000000.0) / (HEAD_DIM // 2)))
    angles = (token - start).astype(jnp.float32) * frequency
    cos_ref[...] = jnp.cos(angles)
    sin_ref[...] = jnp.where(lane < HEAD_DIM // 2, -1.0, 1.0) * jnp.sin(angles)

    def turn(x, cos_part, sin_part):
        wide = x.astype(jnp.float32)
        swapped = pltpu.roll(wide, HEAD_DIM // 2, 1)
        return (wide * cos_part + swapped * sin_part).astype(jnp.bfloat16)

    own[1].wait()
    for head in range(kv_heads):
        columns = slice(head * HEAD_DIM, (head + 1) * HEAD_DIM)
        k_all[me, :, columns] = turn(k_ref[:, columns], cos_ref[...], sin_ref[...])
    @pl.when(passed_on(me))
    def _():
        send(0, 0).start()

    own[2].wait()
    for half in range(halves):
        part = slice(half * HALF, (half + 1) * HALF)
        for head in range(kv_heads * group):
            columns = slice(head * HEAD_DIM, (head + 1) * HEAD_DIM)
            q_rot[half, head // 2, head % 2 * HALF : (head % 2 + 1) * HALF] = turn(
                q_ref[part, columns], cos_ref[part], sin_ref[part]
            )

    pairs = kv_heads * group // 2
    columns_of = [
        slice(2 * pair // group * HEAD_DIM, (2 * pair // group + 1) * HEAD_DIM)
        for pair in range(pairs)
    ]

    def mask(half, source, upto):
        part = slice(half * HALF, (half + 1) * HALF)
        key = source * rows + lax.broadcasted_iota(jnp.int32, (upto, 1), 0)
        query = first_row + half * HALF + lax.broadcasted_iota(jnp.int32, (1, HALF), 1)
        allowed = (key >= start_ref[:, part]) & (key <= query)
        return jnp.concatenate([allowed, allowed], axis=1)

    def weigh(half, source, upto, first, allowed=None):
        for pair in range(pairs):
            found = lax.dot_general(
                k_all[source, :upto, columns_of[pair]],
                q_rot[half, pair],
                (((1,), (1,)), ((), ())),
                preferred_element_type=jnp.float32,
            )
            if allowed is not None:
                found = jnp.where(allowed, found, MASKED)
            peak = jnp.max(found, axis=0, keepdims=True)
            if not first:
                old = top[half, pair]
                peak = jnp.maximum(old, peak)
            weight = jnp.exp2((found - peak) * EXPONENT)
            part = jnp.sum(weight, axis=0, keepdims=True)
            if not first:
                factor = jnp.exp2((old - peak) * EXPONENT)
                shrink[half, pair] = factor
                part += total[half, pair] * factor
            top[half, pair] = peak
            total[half, pair] = part
            weights[half, pair, :upto] = weight.astype(jnp.bfloat16)

    def mix(half, upto, first):
        for pair in range(pairs):
            part = jnp.dot(
                v_turned[columns_of[pair], :upto],
                weights[half, pair, :upto],
                preferred_element_type=jnp.float32,
            )
            acc[half, pair] = part if first else acc[half, pair] * shrink[half, pair] + part

    def finish(half):
        part = slice(half * HALF, (half + 1) * HALF)
        for pair in range(pairs):
            found = (acc[half, pair] * (1.0 / total[half, pair])).astype(jnp.bfloat16).T
            for side in range(2):
                head = 2 * pair + side
                columns = slice(head * HEAD_DIM, (head + 1) * HEAD_DIM)
                out_ref[part, columns] = found[side * HALF : (side + 1) * HALF]

    lows = [first_key_block(me * halves + half, doc0) for half in range(halves)]

    for half in range(halves):
        weigh(half, me, (half + 1) * HALF, True, mask(half, me, (half + 1) * HALF))
    own[3].wait()
    v_turned[...] = v_all[me].T
    for half in range(halves):
        mix(half, (half + 1) * HALF, True)

        @pl.when(lows[half] >= me * halves)
        def _():
            finish(half)

    def absorb(step, carry):
        source = me - step

        def arrived(kind, ref):
            return pltpu.make_async_remote_copy(
                src_ref=ref.at[source],
                dst_ref=ref.at[source],
                send_sem=send_sem.at[step, kind],
                recv_sem=recv_sem.at[step, kind],
                device_id={"seq": lax.rem(me + 1, n)},
                device_id_type=MESH,
            )

        arrived(0, k_all).wait_recv()

        @pl.when(passed_on(source))
        def _():
            send(step, 0).start()
            arrived(1, v_all).wait_recv()
            send(step, 1).start()

        for half in range(halves):
            seen = (source + 1) * halves > lows[half]
            inside = me * halves + half < doc0 // HALF

            @pl.when(seen & inside)
            def _():
                weigh(half, source, rows, False)

            @pl.when(seen & jnp.logical_not(inside))
            def _():
                weigh(half, source, rows, False, mask(half, source, rows))

        @pl.when(jnp.logical_not(passed_on(source)))
        def _():
            arrived(1, v_all).wait_recv()

        v_turned[...] = v_all[source].T
        for half in range(halves):
            @pl.when((source + 1) * halves > lows[half])
            def _():
                mix(half, rows, False)

        return carry

    lax.fori_loop(1, me - first_source(me) + 1, absorb, 0)

    for half in range(halves):
        @pl.when(lows[half] < me * halves)
        def _():
            finish(half)

    @pl.when(passed_on(me))
    def _():
        send(0, 1).wait_send()
        send(0, 0).wait_send()

    def sent(step, carry):
        @pl.when(passed_on(me - step))
        def _():
            send(step, 0).wait_send()
            send(step, 1).wait_send()

        return carry

    lax.fori_loop(1, me - first_source(me) + 1, sent, 0)


def shards(n, queries, keys, values, segments):
    rows = queries.shape[0]
    tokens = n * rows
    doc0 = tokens // 2 + HALF
    kv_heads = keys.shape[1] // HEAD_DIM
    heads = queries.shape[1] // HEAD_DIM
    halves = rows // HALF
    operands = [
        pltpu.with_memory_space_constraint(operand, pltpu.HBM)
        for operand in (queries, keys, values, segments.reshape(1, rows))
    ]
    specs = [pl.BlockSpec(memory_space=pltpu.HBM)] * 4
    has_before = (doc0 + SECOND_DOC) // rows < n - 1
    if has_before:
        every = lax.all_gather(segments, "seq", axis=0, tiled=True)
        before = jnp.sum((every < segments[0]).astype(jnp.int32))
        operands.append(before.reshape(1, 1))
        specs.append(pl.BlockSpec(memory_space=pltpu.SMEM))
    return pl.pallas_call(
        functools.partial(kernel, n, doc0, has_before),
        out_shape=jax.ShapeDtypeStruct(queries.shape, jnp.bfloat16),
        in_specs=specs,
        out_specs=pl.BlockSpec(memory_space=pltpu.VMEM),
        scratch_shapes=[
            pltpu.VMEM(queries.shape, jnp.bfloat16),
            pltpu.VMEM(keys.shape, jnp.bfloat16),
            pltpu.VMEM((1, rows), jnp.int32),
            pltpu.VMEM((n, rows, kv_heads * HEAD_DIM), jnp.bfloat16),
            pltpu.VMEM((n, rows, kv_heads * HEAD_DIM), jnp.bfloat16),
            pltpu.VMEM((halves, heads // 2, 2 * HALF, HEAD_DIM), jnp.bfloat16),
            pltpu.VMEM((halves, heads // 2, HEAD_DIM, 2 * HALF), jnp.float32),
            pltpu.VMEM((halves, heads // 2, 1, 2 * HALF), jnp.float32),
            pltpu.VMEM((halves, heads // 2, 1, 2 * HALF), jnp.float32),
            pltpu.VMEM((rows, HEAD_DIM), jnp.float32),
            pltpu.VMEM((rows, HEAD_DIM), jnp.float32),
            pltpu.VMEM((1, rows), jnp.int32),
            pltpu.VMEM((kv_heads * HEAD_DIM, rows), jnp.bfloat16),
            pltpu.VMEM((halves, heads // 2, rows, 2 * HALF), jnp.bfloat16),
            pltpu.VMEM((halves, heads // 2, 1, 2 * HALF), jnp.float32),
            pltpu.SemaphoreType.DMA((n + 1, 2)),
            pltpu.SemaphoreType.DMA((n + 1, 2)),
            pltpu.SemaphoreType.DMA((4,)),
        ],
        compiler_params=pltpu.CompilerParams(
            collective_id=0, has_side_effects=True, vmem_limit_bytes=48 * 1024 * 1024
        ),
    )(*operands)


def solution(mesh):
    placed = (
        P(("rep", "seq"), "tp"),
        P(("rep", "seq"), "tp"),
        P(("rep", "seq"), "tp"),
        P(("rep", "seq")),
    )
    return jax.shard_map(
        functools.partial(shards, mesh.shape["seq"]),
        mesh=mesh,
        in_specs=placed,
        out_specs=P(("rep", "seq"), "tp"),
        check_vma=False,
    )
```

```python
import functools
import math

import jax
import jax.numpy as jnp
from jax import lax
from jax.experimental import pallas as pl
from jax.experimental.pallas import tpu as pltpu
from jax.sharding import PartitionSpec as P

HEAD_DIM = 128
HALF = 128
SECOND_DOC = 192
MASKED = -1e30
EXPONENT = math.log2(math.e) / math.sqrt(HEAD_DIM)
MESH = pl.DeviceIdType.MESH


def first_key_block(tile, doc0):
    later = jnp.where(tile < (doc0 + SECOND_DOC) // HALF + 1, doc0 // HALF, (doc0 + SECOND_DOC) // HALF)
    return jnp.where(tile < doc0 // HALF, 0, later)


def kernel(
    n, doc0, has_before, q_hbm, k_hbm, v_hbm, seg_hbm, *refs
):
    before_ref = refs[0] if has_before else None
    (
        out_ref, q_ref, k_ref, seg_ref, k_all, v_all, q_rot, acc, top, total,
        cos_ref, sin_ref, start_ref, v_turned, weights, shrink, send_sem, recv_sem, own_sem,
    ) = refs[has_before:]
    me = lax.axis_index("seq")
    rows = k_hbm.shape[0]
    halves = rows // HALF
    kv_heads = k_hbm.shape[1] // HEAD_DIM
    group = q_hbm.shape[1] // k_hbm.shape[1]
    first_row = me * rows

    barrier = pltpu.get_barrier_semaphore()

    def first_source(device):
        low = first_key_block(device * halves, doc0)
        for half in range(1, halves):
            low = jnp.minimum(low, first_key_block(device * halves + half, doc0))
        return low // halves

    def passed_on(source):
        return (me + 1 < n) & (source >= first_source(me + 1))

    def receives():
        return first_source(me) < me

    @pl.when(receives())
    def _():
        pl.semaphore_signal(
            barrier, inc=1, device_id={"seq": lax.rem(me - 1 + n, n)}, device_id_type=MESH
        )

    def head_columns(head):
        return slice(head * HEAD_DIM, (head + 1) * HEAD_DIM)

    own = [
        pltpu.make_async_copy(source, target, own_sem.at[place])
        for place, (source, target) in enumerate(
            [(seg_hbm, seg_ref), (k_hbm, k_ref), (q_hbm, q_ref)]
            + [(v_hbm.at[:, head_columns(kv)], v_all.at[me, kv]) for kv in range(kv_heads)]
        )
    ]
    for copy in own[3:] + own[:3]:
        copy.start()

    def send(step, held, kind, kv):
        return pltpu.make_async_remote_copy(
            src_ref=held.at[me - step, kv],
            dst_ref=held.at[me - step, kv],
            send_sem=send_sem.at[step + 1, kind, kv],
            recv_sem=recv_sem.at[step + 1, kind, kv],
            device_id={"seq": lax.rem(me + 1, n)},
            device_id_type=MESH,
        )

    def arrived(step, held, kind, kv):
        return pltpu.make_async_remote_copy(
            src_ref=held.at[me - step, kv],
            dst_ref=held.at[me - step, kv],
            send_sem=send_sem.at[step, kind, kv],
            recv_sem=recv_sem.at[step, kind, kv],
            device_id={"seq": lax.rem(me + 1, n)},
            device_id_type=MESH,
        )

    for copy in own[3:]:
        copy.wait()

    @pl.when(passed_on(me))
    def _():
        pl.semaphore_wait(barrier, 1)
        for kv in range(kv_heads):
            send(0, v_all, 1, kv).start()

    own[0].wait()
    seg_row = jnp.broadcast_to(seg_ref[...], (rows, rows))
    seg_column = seg_row.T

    def document_start(token, earlier, axis):
        count = jnp.sum(earlier.astype(jnp.float32), axis=axis, keepdims=True).astype(jnp.int32)
        start = first_row + count
        if has_before:
            start = jnp.where(count == 0, before_ref[0, 0], start)
        return jnp.where(token < doc0, 0, jnp.where(token < doc0 + SECOND_DOC, doc0, start))

    token = first_row + lax.broadcasted_iota(jnp.int32, (1, rows), 1)
    start_ref[...] = document_start(token, seg_column < seg_row, 0)
    token = first_row + lax.broadcasted_iota(jnp.int32, (rows, 1), 0)
    start = document_start(token, seg_row < seg_column, 1)
    lane = lax.broadcasted_iota(jnp.int32, (1, HEAD_DIM), 1)
    index = (lane % (HEAD_DIM // 2)).astype(jnp.float32)
    frequency = jnp.exp(index * (-math.log(1000000.0) / (HEAD_DIM // 2)))
    angles = (token - start).astype(jnp.float32) * frequency
    cos_ref[...] = jnp.cos(angles)
    sin_ref[...] = jnp.where(lane < HEAD_DIM // 2, -1.0, 1.0) * jnp.sin(angles)

    def turn(x, cos_part, sin_part):
        wide = x.astype(jnp.float32)
        swapped = pltpu.roll(wide, HEAD_DIM // 2, 1)
        return (wide * cos_part + swapped * sin_part).astype(jnp.bfloat16)

    own[1].wait()
    for kv in range(kv_heads):
        k_all[me, kv] = turn(k_ref[:, head_columns(kv)], cos_ref[...], sin_ref[...])

        @pl.when(passed_on(me))
        def _():
            send(0, k_all, 0, kv).start()

    own[2].wait()
    for half in range(halves):
        part = slice(half * HALF, (half + 1) * HALF)
        for head in range(kv_heads * group):
            columns = slice(head * HEAD_DIM, (head + 1) * HEAD_DIM)
            q_rot[half, head // 2, head % 2 * HALF : (head % 2 + 1) * HALF] = turn(
                q_ref[part, columns], cos_ref[part], sin_ref[part]
            )

    pairs = kv_heads * group // 2
    per_kv = group // 2

    def mask(half, source, upto):
        part = slice(half * HALF, (half + 1) * HALF)
        key = source * rows + lax.broadcasted_iota(jnp.int32, (upto, 1), 0)
        query = first_row + half * HALF + lax.broadcasted_iota(jnp.int32, (1, HALF), 1)
        allowed = (key >= start_ref[:, part]) & (key <= query)
        return jnp.concatenate([allowed, allowed], axis=1)

    def weigh(half, source, upto, first, allowed=None):
        for pair in range(pairs):
            found = lax.dot_general(
                k_all[source, pair // per_kv, :upto],
                q_rot[half, pair],
                (((1,), (1,)), ((), ())),
                preferred_element_type=jnp.float32,
            )
            if allowed is not None:
                found = jnp.where(allowed, found, MASKED)
            peak = jnp.max(found, axis=0, keepdims=True)
            if not first:
                old = top[half, pair]
                peak = jnp.maximum(old, peak)
            weight = jnp.exp2((found - peak) * EXPONENT)
            part = jnp.sum(weight, axis=0, keepdims=True)
            if not first:
                factor = jnp.exp2((old - peak) * EXPONENT)
                shrink[half, pair] = factor
                part += total[half, pair] * factor
            top[half, pair] = peak
            total[half, pair] = part
            weights[half, pair, :upto] = weight.astype(jnp.bfloat16)

    def mix(half, kv, upto, first):
        for pair in range(kv * per_kv, (kv + 1) * per_kv):
            part = jnp.dot(
                v_turned[kv, :, :upto],
                weights[half, pair, :upto],
                preferred_element_type=jnp.float32,
            )
            acc[half, pair] = part if first else acc[half, pair] * shrink[half, pair] + part

    def finish(half, kv):
        part = slice(half * HALF, (half + 1) * HALF)
        for pair in range(kv * per_kv, (kv + 1) * per_kv):
            found = (acc[half, pair] * (1.0 / total[half, pair])).astype(jnp.bfloat16).T
            for side in range(2):
                head = 2 * pair + side
                columns = slice(head * HEAD_DIM, (head + 1) * HEAD_DIM)
                out_ref[part, columns] = found[side * HALF : (side + 1) * HALF]

    lows = [first_key_block(me * halves + half, doc0) for half in range(halves)]

    for half in range(halves):
        weigh(half, me, (half + 1) * HALF, True, mask(half, me, (half + 1) * HALF))
    for kv in range(kv_heads):
        v_turned[kv] = v_all[me, kv].T
        for half in range(halves):
            mix(half, kv, (half + 1) * HALF, True)

            @pl.when(lows[half] >= me * halves)
            def _():
                finish(half, kv)

    def absorb(step, carry):
        source = me - step

        for kv in range(kv_heads):
            arrived(step, k_all, 0, kv).wait_recv()

        @pl.when(passed_on(source))
        def _():
            for kv in range(kv_heads):
                send(step, k_all, 0, kv).start()
            for kv in range(kv_heads):
                arrived(step, v_all, 1, kv).wait_recv()
                send(step, v_all, 1, kv).start()

        for half in range(halves):
            seen = (source + 1) * halves > lows[half]
            inside = me * halves + half < doc0 // HALF

            @pl.when(seen & inside)
            def _():
                weigh(half, source, rows, False)

            @pl.when(seen & jnp.logical_not(inside))
            def _():
                weigh(half, source, rows, False, mask(half, source, rows))

        for kv in range(kv_heads):
            @pl.when(jnp.logical_not(passed_on(source)))
            def _():
                arrived(step, v_all, 1, kv).wait_recv()

            v_turned[kv] = v_all[source, kv].T
            for half in range(halves):
                @pl.when((source + 1) * halves > lows[half])
                def _():
                    mix(half, kv, rows, False)

                last = lows[half] // halves == source

                @pl.when(last)
                def _():
                    finish(half, kv)

        return carry

    lax.fori_loop(1, me - first_source(me) + 1, absorb, 0)

    @pl.when(passed_on(me))
    def _():
        for kv in range(kv_heads):
            send(0, v_all, 1, kv).wait_send()
            send(0, k_all, 0, kv).wait_send()

    def sent(step, carry):
        @pl.when(passed_on(me - step))
        def _():
            for kv in range(kv_heads):
                send(step, k_all, 0, kv).wait_send()
                send(step, v_all, 1, kv).wait_send()

        return carry

    lax.fori_loop(1, me - first_source(me) + 1, sent, 0)


def shards(n, queries, keys, values, segments):
    rows = queries.shape[0]
    tokens = n * rows
    doc0 = tokens // 2 + HALF
    kv_heads = keys.shape[1] // HEAD_DIM
    heads = queries.shape[1] // HEAD_DIM
    halves = rows // HALF
    operands = [
        pltpu.with_memory_space_constraint(operand, pltpu.HBM)
        for operand in (queries, keys, values, segments.reshape(1, rows))
    ]
    specs = [pl.BlockSpec(memory_space=pltpu.HBM)] * 4
    has_before = (doc0 + SECOND_DOC) // rows < n - 1
    if has_before:
        every = lax.all_gather(segments, "seq", axis=0, tiled=True)
        before = jnp.sum((every < segments[0]).astype(jnp.int32))
        operands.append(before.reshape(1, 1))
        specs.append(pl.BlockSpec(memory_space=pltpu.SMEM))
    return pl.pallas_call(
        functools.partial(kernel, n, doc0, has_before),
        out_shape=jax.ShapeDtypeStruct(queries.shape, jnp.bfloat16),
        in_specs=specs,
        out_specs=pl.BlockSpec(memory_space=pltpu.VMEM),
        scratch_shapes=[
            pltpu.VMEM(queries.shape, jnp.bfloat16),
            pltpu.VMEM(keys.shape, jnp.bfloat16),
            pltpu.VMEM((1, rows), jnp.int32),
            pltpu.VMEM((n, kv_heads, rows, HEAD_DIM), jnp.bfloat16),
            pltpu.VMEM((n, kv_heads, rows, HEAD_DIM), jnp.bfloat16),
            pltpu.VMEM((halves, heads // 2, 2 * HALF, HEAD_DIM), jnp.bfloat16),
            pltpu.VMEM((halves, heads // 2, HEAD_DIM, 2 * HALF), jnp.float32),
            pltpu.VMEM((halves, heads // 2, 1, 2 * HALF), jnp.float32),
            pltpu.VMEM((halves, heads // 2, 1, 2 * HALF), jnp.float32),
            pltpu.VMEM((rows, HEAD_DIM), jnp.float32),
            pltpu.VMEM((rows, HEAD_DIM), jnp.float32),
            pltpu.VMEM((1, rows), jnp.int32),
            pltpu.VMEM((kv_heads, HEAD_DIM, rows), jnp.bfloat16),
            pltpu.VMEM((halves, heads // 2, rows, 2 * HALF), jnp.bfloat16),
            pltpu.VMEM((halves, heads // 2, 1, 2 * HALF), jnp.float32),
            pltpu.SemaphoreType.DMA((n + 1, 2, kv_heads)),
            pltpu.SemaphoreType.DMA((n + 1, 2, kv_heads)),
            pltpu.SemaphoreType.DMA((3 + kv_heads,)),
        ],
        compiler_params=pltpu.CompilerParams(
            collective_id=0, has_side_effects=True, vmem_limit_bytes=48 * 1024 * 1024
        ),
    )(*operands)


def solution(mesh):
    placed = (
        P(("rep", "seq"), "tp"),
        P(("rep", "seq"), "tp"),
        P(("rep", "seq"), "tp"),
        P(("rep", "seq")),
    )
    return jax.shard_map(
        functools.partial(shards, mesh.shape["seq"]),
        mesh=mesh,
        in_specs=placed,
        out_specs=P(("rep", "seq"), "tp"),
        check_vma=False,
    )
```

```python
import functools
import math

import jax
import jax.numpy as jnp
from jax import lax
from jax.experimental import pallas as pl
from jax.experimental.pallas import tpu as pltpu
from jax.sharding import PartitionSpec as P

HEAD_DIM = 128
HALF = 128
SECOND_DOC = 192
MASKED = -1e30
EXPONENT = math.log2(math.e) / math.sqrt(HEAD_DIM)
MESH = pl.DeviceIdType.MESH


def first_key_block(tile, doc0):
    later = jnp.where(tile < (doc0 + SECOND_DOC) // HALF + 1, doc0 // HALF, (doc0 + SECOND_DOC) // HALF)
    return jnp.where(tile < doc0 // HALF, 0, later)


def kernel(
    n, doc0, has_before, q_hbm, k_hbm, v_hbm, seg_hbm, *refs
):
    before_ref = refs[0] if has_before else None
    (
        out_ref, q_ref, k_ref, seg_ref, k_all, v_all, q_rot, acc, top, total,
        cos_ref, sin_ref, start_ref, v_turned, weights, shrink, send_sem, recv_sem, own_sem,
    ) = refs[has_before:]
    me = lax.axis_index("seq")
    rows = k_hbm.shape[0]
    halves = rows // HALF
    kv_heads = k_hbm.shape[1] // HEAD_DIM
    group = q_hbm.shape[1] // k_hbm.shape[1]
    first_row = me * rows

    barrier = pltpu.get_barrier_semaphore()

    def first_source(device):
        low = first_key_block(device * halves, doc0)
        for half in range(1, halves):
            low = jnp.minimum(low, first_key_block(device * halves + half, doc0))
        return low // halves

    def passed_on(source):
        return (me + 1 < n) & (source >= first_source(me + 1))

    def receives():
        return first_source(me) < me

    def head_columns(head):
        return slice(head * HEAD_DIM, (head + 1) * HEAD_DIM)

    own = [
        pltpu.make_async_copy(source, target, own_sem.at[place])
        for place, (source, target) in enumerate(
            [(seg_hbm, seg_ref), (k_hbm, k_ref), (q_hbm, q_ref)]
            + [(v_hbm.at[:, head_columns(kv)], v_all.at[me, kv]) for kv in range(kv_heads)]
        )
    ]
    for copy in own[3:] + own[:2]:
        copy.start()

    @pl.when(receives())
    def _():
        pl.semaphore_signal(
            barrier, inc=1, device_id={"seq": lax.rem(me - 1 + n, n)}, device_id_type=MESH
        )

    def send(step, held, kind, kv):
        return pltpu.make_async_remote_copy(
            src_ref=held.at[me - step] if kv is None else held.at[me - step, kv],
            dst_ref=held.at[me - step] if kv is None else held.at[me - step, kv],
            send_sem=send_sem.at[step + 1, kind, kv or 0],
            recv_sem=recv_sem.at[step + 1, kind, kv or 0],
            device_id={"seq": lax.rem(me + 1, n)},
            device_id_type=MESH,
        )

    def arrived(step, held, kind, kv):
        return pltpu.make_async_remote_copy(
            src_ref=held.at[me - step] if kv is None else held.at[me - step, kv],
            dst_ref=held.at[me - step] if kv is None else held.at[me - step, kv],
            send_sem=send_sem.at[step, kind, kv or 0],
            recv_sem=recv_sem.at[step, kind, kv or 0],
            device_id={"seq": lax.rem(me + 1, n)},
            device_id_type=MESH,
        )

    own[2].start()
    for copy in own[3:]:
        copy.wait()

    @pl.when(passed_on(me))
    def _():
        pl.semaphore_wait(barrier, 1)
        for kv in range(kv_heads):
            send(0, v_all, 1, kv).start()

    own[0].wait()
    seg_row = jnp.broadcast_to(seg_ref[...], (rows, rows))
    seg_column = seg_row.T

    def document_start(token, earlier, axis):
        count = jnp.sum(earlier.astype(jnp.float32), axis=axis, keepdims=True).astype(jnp.int32)
        start = first_row + count
        if has_before:
            start = jnp.where(count == 0, before_ref[0, 0], start)
        return jnp.where(token < doc0, 0, jnp.where(token < doc0 + SECOND_DOC, doc0, start))

    token = first_row + lax.broadcasted_iota(jnp.int32, (1, rows), 1)
    start_ref[...] = document_start(token, seg_column < seg_row, 0)
    token = first_row + lax.broadcasted_iota(jnp.int32, (rows, 1), 0)
    start = document_start(token, seg_row < seg_column, 1)
    lane = lax.broadcasted_iota(jnp.int32, (1, HEAD_DIM), 1)
    index = (lane % (HEAD_DIM // 2)).astype(jnp.float32)
    frequency = jnp.exp(index * (-math.log(1000000.0) / (HEAD_DIM // 2)))
    angles = (token - start).astype(jnp.float32) * frequency
    cos_ref[...] = jnp.cos(angles)
    sin_ref[...] = jnp.where(lane < HEAD_DIM // 2, -1.0, 1.0) * jnp.sin(angles)

    def turn(x, cos_part, sin_part):
        wide = x.astype(jnp.float32)
        swapped = pltpu.roll(wide, HEAD_DIM // 2, 1)
        return (wide * cos_part + swapped * sin_part).astype(jnp.bfloat16)

    own[1].wait()
    for kv in range(kv_heads):
        k_all[me, kv] = turn(k_ref[:, head_columns(kv)], cos_ref[...], sin_ref[...])

    @pl.when(passed_on(me))
    def _():
        send(0, k_all, 0, None).start()

    own[2].wait()
    for half in range(halves):
        part = slice(half * HALF, (half + 1) * HALF)
        for head in range(kv_heads * group):
            columns = slice(head * HEAD_DIM, (head + 1) * HEAD_DIM)
            q_rot[half, head // 2, head % 2 * HALF : (head % 2 + 1) * HALF] = turn(
                q_ref[part, columns], cos_ref[part], sin_ref[part]
            )

    pairs = kv_heads * group // 2
    per_kv = group // 2

    def mask(half, source, upto):
        part = slice(half * HALF, (half + 1) * HALF)
        key = source * rows + lax.broadcasted_iota(jnp.int32, (upto, 1), 0)
        query = first_row + half * HALF + lax.broadcasted_iota(jnp.int32, (1, HALF), 1)
        allowed = (key >= start_ref[:, part]) & (key <= query)
        return jnp.concatenate([allowed, allowed], axis=1)

    def weigh(half, source, upto, first, allowed=None):
        for pair in range(pairs):
            found = lax.dot_general(
                k_all[source, pair // per_kv, :upto],
                q_rot[half, pair],
                (((1,), (1,)), ((), ())),
                preferred_element_type=jnp.float32,
            )
            if allowed is not None:
                found = jnp.where(allowed, found, MASKED)
            peak = jnp.max(found, axis=0, keepdims=True)
            if not first:
                old = top[half, pair]
                peak = jnp.maximum(old, peak)
            weight = jnp.exp2((found - peak) * EXPONENT)
            part = jnp.sum(weight, axis=0, keepdims=True)
            if not first:
                factor = jnp.exp2((old - peak) * EXPONENT)
                shrink[half, pair] = factor
                part += total[half, pair] * factor
            top[half, pair] = peak
            total[half, pair] = part
            weights[half, pair, :upto] = weight.astype(jnp.bfloat16)

    def mix(half, kv, upto, first):
        for pair in range(kv * per_kv, (kv + 1) * per_kv):
            part = jnp.dot(
                v_turned[kv, :, :upto],
                weights[half, pair, :upto],
                preferred_element_type=jnp.float32,
            )
            acc[half, pair] = part if first else acc[half, pair] * shrink[half, pair] + part

    def finish(half, kv):
        part = slice(half * HALF, (half + 1) * HALF)
        for pair in range(kv * per_kv, (kv + 1) * per_kv):
            found = (acc[half, pair] * (1.0 / total[half, pair])).astype(jnp.bfloat16).T
            for side in range(2):
                head = 2 * pair + side
                columns = slice(head * HEAD_DIM, (head + 1) * HEAD_DIM)
                out_ref[part, columns] = found[side * HALF : (side + 1) * HALF]

    lows = [first_key_block(me * halves + half, doc0) for half in range(halves)]

    for half in range(halves):
        weigh(half, me, (half + 1) * HALF, True, mask(half, me, (half + 1) * HALF))
    for kv in range(kv_heads):
        v_turned[kv] = v_all[me, kv].T
        for half in range(halves):
            mix(half, kv, (half + 1) * HALF, True)

            @pl.when(lows[half] >= me * halves)
            def _():
                finish(half, kv)

    def absorb(step, carry):
        source = me - step

        arrived(step, k_all, 0, None).wait_recv()

        @pl.when(passed_on(source))
        def _():
            send(step, k_all, 0, None).start()
            for kv in range(kv_heads):
                arrived(step, v_all, 1, kv).wait_recv()
                send(step, v_all, 1, kv).start()

        for half in range(halves):
            seen = (source + 1) * halves > lows[half]
            inside = me * halves + half < doc0 // HALF

            @pl.when(seen & inside)
            def _():
                weigh(half, source, rows, False)

            @pl.when(seen & jnp.logical_not(inside))
            def _():
                weigh(half, source, rows, False, mask(half, source, rows))

        for kv in range(kv_heads):
            @pl.when(jnp.logical_not(passed_on(source)))
            def _():
                arrived(step, v_all, 1, kv).wait_recv()

            v_turned[kv] = v_all[source, kv].T
            for half in range(halves):
                @pl.when((source + 1) * halves > lows[half])
                def _():
                    mix(half, kv, rows, False)

                last = lows[half] // halves == source

                @pl.when(last)
                def _():
                    finish(half, kv)

        return carry

    lax.fori_loop(1, me - first_source(me) + 1, absorb, 0)

    @pl.when(passed_on(me))
    def _():
        for kv in range(kv_heads):
            send(0, v_all, 1, kv).wait_send()
        send(0, k_all, 0, None).wait_send()

    def sent(step, carry):
        @pl.when(passed_on(me - step))
        def _():
            send(step, k_all, 0, None).wait_send()
            for kv in range(kv_heads):
                send(step, v_all, 1, kv).wait_send()

        return carry

    lax.fori_loop(1, me - first_source(me) + 1, sent, 0)


def shards(n, queries, keys, values, segments):
    rows = queries.shape[0]
    tokens = n * rows
    doc0 = tokens // 2 + HALF
    kv_heads = keys.shape[1] // HEAD_DIM
    heads = queries.shape[1] // HEAD_DIM
    halves = rows // HALF
    operands = [
        pltpu.with_memory_space_constraint(operand, pltpu.HBM)
        for operand in (queries, keys, values, segments.reshape(1, rows))
    ]
    specs = [pl.BlockSpec(memory_space=pltpu.HBM)] * 4
    has_before = (doc0 + SECOND_DOC) // rows < n - 1
    if has_before:
        every = lax.all_gather(segments, "seq", axis=0, tiled=True)
        before = jnp.sum((every < segments[0]).astype(jnp.int32))
        operands.append(before.reshape(1, 1))
        specs.append(pl.BlockSpec(memory_space=pltpu.SMEM))
    return pl.pallas_call(
        functools.partial(kernel, n, doc0, has_before),
        out_shape=jax.ShapeDtypeStruct(queries.shape, jnp.bfloat16),
        in_specs=specs,
        out_specs=pl.BlockSpec(memory_space=pltpu.VMEM),
        scratch_shapes=[
            pltpu.VMEM(queries.shape, jnp.bfloat16),
            pltpu.VMEM(keys.shape, jnp.bfloat16),
            pltpu.VMEM((1, rows), jnp.int32),
            pltpu.VMEM((n, kv_heads, rows, HEAD_DIM), jnp.bfloat16),
            pltpu.VMEM((n, kv_heads, rows, HEAD_DIM), jnp.bfloat16),
            pltpu.VMEM((halves, heads // 2, 2 * HALF, HEAD_DIM), jnp.bfloat16),
            pltpu.VMEM((halves, heads // 2, HEAD_DIM, 2 * HALF), jnp.float32),
            pltpu.VMEM((halves, heads // 2, 1, 2 * HALF), jnp.float32),
            pltpu.VMEM((halves, heads // 2, 1, 2 * HALF), jnp.float32),
            pltpu.VMEM((rows, HEAD_DIM), jnp.float32),
            pltpu.VMEM((rows, HEAD_DIM), jnp.float32),
            pltpu.VMEM((1, rows), jnp.int32),
            pltpu.VMEM((kv_heads, HEAD_DIM, rows), jnp.bfloat16),
            pltpu.VMEM((halves, heads // 2, rows, 2 * HALF), jnp.bfloat16),
            pltpu.VMEM((halves, heads // 2, 1, 2 * HALF), jnp.float32),
            pltpu.SemaphoreType.DMA((n + 1, 2, kv_heads)),
            pltpu.SemaphoreType.DMA((n + 1, 2, kv_heads)),
            pltpu.SemaphoreType.DMA((3 + kv_heads,)),
        ],
        compiler_params=pltpu.CompilerParams(
            collective_id=0, has_side_effects=True, vmem_limit_bytes=48 * 1024 * 1024
        ),
    )(*operands)


def solution(mesh):
    placed = (
        P(("rep", "seq"), "tp"),
        P(("rep", "seq"), "tp"),
        P(("rep", "seq"), "tp"),
        P(("rep", "seq")),
    )
    return jax.shard_map(
        functools.partial(shards, mesh.shape["seq"]),
        mesh=mesh,
        in_specs=placed,
        out_specs=P(("rep", "seq"), "tp"),
        check_vma=False,
    )
```
